32 devices in a mesh: dp: 16 (over z, y, x), tensor: 2 (over core).
Axes of the slice: x: 2, y: 2, z: 4, core: 2. Of those that a mesh axis runs over, the one named last changes fastest.
Arguments:
- hidden_in: bfloat16 [32768, 768], P(('dp', 'tensor')), may hold values from -6 to 6
- out_grad: bfloat16 [32768, 768], P(('dp', 'tensor')), may hold values from -6 to 6
- seq_lengths: int32 [16, 8], P('dp'), may hold values from 1 to 1024, as said below
- attn_gain: bfloat16 [768], P('dp'), may hold values from 0.099609375 to 1.8984375
- attn_shift: bfloat16 [768], P('dp'), may hold values from -1.75 to 1.75
- mlp_gain: bfloat16 [768], P('dp'), may hold values from 0.099609375 to 1.8984375
- mlp_shift: bfloat16 [768], P('dp'), may hold values from -1.75 to 1.75
- qkv_weight: bfloat16 [768, 12, 192], P('dp', 'tensor'), may hold values from -0.21875 to 0.21875
- qkv_bias: bfloat16 [2304], P('dp'), may hold values from -1.75 to 1.75
- dense_weight: bfloat16 [768, 12, 64], P('dp', 'tensor'), may hold values from -0.875 to 0.875
- dense_bias: bfloat16 [768], P('dp'), may hold values from -1.75 to 1.75
- fc_weight: bfloat16 [768, 3072], P('dp', 'tensor'), may hold values from -0.21875 to 0.21875
- fc_bias: bfloat16 [3072], P('dp'), may hold values from -1.75 to 1.75
- proj_weight: bfloat16 [768, 3072], P('dp', 'tensor'), may hold values from -0.15625 to 0.15625
- proj_bias: bfloat16 [768], P('dp'), may hold values from -1.75 to 1.75
Outputs:
- block_out: bfloat16 [32768, 768], P(('dp', 'tensor'))
- input_grad: float32 [32768, 768], P(('dp', 'tensor'))
- attn_gain_grad: float32 [768], P(('dp', 'tensor'))
- attn_shift_grad: float32 [768], P(('dp', 'tensor'))
- mlp_gain_grad: float32 [768], P(('dp', 'tensor'))
- mlp_shift_grad: float32 [768], P(('dp', 'tensor'))
- qkv_weight_grad: float32 [768, 12, 192], P('dp', 'tensor')
- qkv_bias_grad: float32 [2304], P(('dp', 'tensor'))
- dense_weight_grad: float32 [768, 12, 64], P('dp', 'tensor')
- dense_bias_grad: float32 [768], P(('dp', 'tensor'))
- fc_weight_grad: float32 [768, 3072], P('dp', 'tensor')
- fc_bias_grad: float32 [3072], P(('dp', 'tensor'))
- proj_weight_grad: float32 [768, 3072], P('dp', 'tensor')
- proj_bias_grad: float32 [768], P(('dp', 'tensor'))
The draws below stay inside these ranges and needn't reach their ends.
Inputs may be any that keep to these rules, and one draw needn't show every extreme that they name: `seq_lengths`: row g lists the 8 sequences of group g in order; they are all 1 or longer and sum to 2048. One sequence of each row has exactly 1024 rows and covers rows 1023 and 1024 of its group.
All inputs are finite; a program needn't handle non-finite values.
Results may differ from the reference program's by a relative error of at most 0.012.
Values may be sent and summed in bfloat16 or wider, within the bound.
A program may use at most 256 MiB of HBM per device.

```python
import jax
import jax.numpy as jnp
from jax import lax

D = 768
H = 12
HD = 64
FF = 3072
ROWS = 1024
SEQS = 8
SEQ_MAX = 1024
GRP = 2048
TOKENS = 32768
N_DP = 16
N_TENSOR = 2


def draw_seq_lengths(key, part):
    group_rows = ROWS * N_TENSOR
    longest = min(SEQ_MAX, group_rows - SEQS)
    outer = group_rows - longest
    low_start = max(1, group_rows // 2 - longest + 1)
    high_start = min(outer - 1, group_rows // 2 - 1)

    def one_group(sub_key):
        key_start, key_cuts = jax.random.split(sub_key)
        start_row = jax.random.randint(key_start, (), low_start, high_start + 1).astype(jnp.int32)
        picks = jax.random.permutation(key_cuts, outer - 2)[:SEQS - 3].astype(jnp.int32) + 1
        picks = picks + (picks >= start_row).astype(jnp.int32)
        cut_rows = jnp.where(picks > start_row, picks + longest, picks)
        fixed_rows = jnp.stack([jnp.zeros((), jnp.int32), start_row, start_row + longest, jnp.full((), group_rows, jnp.int32)])
        bounds = jnp.sort(jnp.concatenate([fixed_rows, cut_rows]))
        return (bounds[1:] - bounds[:-1]).astype(jnp.int32)
    return jax.vmap(one_group)(jax.random.split(key, N_DP))


def raised(values, rng, source, target, blocks, factor):
    owner, partner = [(jnp.arange(values.shape[position]) // (values.shape[position] // blocks)).reshape([-1 if axis == position else 1 for axis in range(values.ndim)]) for position in (source, target)]
    chosen = jax.random.permutation(rng, blocks)[partner]
    strong = (owner == chosen) | (owner == (partner + blocks // 2) % blocks)
    return jnp.where(strong, factor * values, values)


def block_levels(own_key, extent, pieces, smallest, largest):
    def one(axis_at, blocks):
        steps = jax.random.uniform(jax.random.fold_in(jax.random.fold_in(own_key, 6), axis_at), (blocks,), jnp.float32, smallest / len(pieces), largest / len(pieces))
        return jnp.repeat(jnp.exp(steps), extent[axis_at] // blocks).reshape((-1,) + (1,) * (len(extent) - axis_at - 1))

    gain = one(*pieces[0])
    for cut in pieces[1:]:
        gain = gain * one(*cut)
    return gain


def scatter_about(own_key, extent, scale, limit, shards=(), held_as=jnp.bfloat16):
    level = block_levels(own_key, extent, shards, -0.22, 0.18) if shards else 1.0
    values = jax.random.normal(own_key, extent, jnp.float32) * scale * level
    return jnp.minimum(jnp.maximum(values, -limit), limit).astype(held_as)


def bell_draw_with(rng, extent, scale, reach, pieces, heavy, held_as=jnp.bfloat16):
    values = scale * jax.random.normal(rng, extent, jnp.float32)
    if pieces:
        values = values * block_levels(rng, extent, pieces, -0.22, 0.18)
    return jnp.clip(raised(values, jax.random.fold_in(rng, 3), *heavy), -reach, reach).astype(held_as)


def setup_inputs(seed: int = 0) -> dict:
    key_of = jax.random.split(jax.random.key(seed), 16)
    return {
        "hidden_in": bell_draw_with(key_of[0], (TOKENS, D), 1.0, 6.0, ((0, 32),), (0, 1, 32, 2.75)),
        "out_grad": bell_draw_with(key_of[1], (TOKENS, D), 1.0, 6.0, ((0, 32),), (0, 1, 32, 2.75)),
        "seq_lengths": draw_seq_lengths(jax.random.fold_in(key_of[15], 71), 0),
        "attn_gain": jnp.clip(1.0 + 0.18 * jax.random.normal(key_of[3], (D,), jnp.float32), 0.099609375, 1.8984375).astype(jnp.bfloat16),
        "attn_shift": scatter_about(key_of[4], (D,), 0.3, 1.75, ((0, 16),)),
        "mlp_gain": jnp.clip(1.0 + 0.18 * jax.random.normal(key_of[5], (D,), jnp.float32), 0.099609375, 1.8984375).astype(jnp.bfloat16),
        "mlp_shift": scatter_about(key_of[6], (D,), 0.3, 1.75, ((0, 16),)),
        "qkv_weight": scatter_about(key_of[7], (D, H, 3 * HD), D ** -0.5, 0.21875, ((0, 16), (1, 2))),
        "qkv_bias": scatter_about(key_of[8], (3 * H * HD,), 0.3, 1.75, ((0, 16),)),
        "dense_weight": scatter_about(key_of[9], (D, H, HD), (H * HD // 16) ** -0.5, 0.875, ((0, 16), (1, 2))),
        "dense_bias": scatter_about(key_of[10], (D,), 0.3, 1.75, ((0, 16),)),
        "fc_weight": scatter_about(key_of[11], (D, FF), D ** -0.5, 0.21875, ((0, 16), (1, 2))),
        "fc_bias": scatter_about(key_of[12], (FF,), 0.3, 1.75, ((0, 16),)),
        "proj_weight": scatter_about(key_of[13], (D, FF), (FF // 2) ** -0.5, 0.15625, ((0, 16), (1, 2))),
        "proj_bias": scatter_about(key_of[14], (D,), 0.3, 1.75, ((0, 16),)),
    }


@jax.custom_vjp
def low(v):
    return lax.optimization_barrier(v.astype(jnp.bfloat16)).astype(jnp.float32)

@jax.custom_vjp
def low_back(v):
    return v

def low_keep(v):
    return (low(v), None)

def low_pass(kept, grad):
    return (grad,)

def back_keep(v):
    return (v, None)

def back_low(kept, grad):
    return (low(grad),)
low.defvjp(low_keep, low_pass)
low_back.defvjp(back_keep, back_low)

def layout(lengths, group_rows):
    seq_ends = jnp.cumsum(lengths).astype(jnp.int32)
    starts = seq_ends - lengths.astype(jnp.int32)
    row_index = jnp.arange(group_rows, dtype=jnp.int32)
    seg_ids = lax.optimization_barrier(jnp.sum((row_index[:, None] >= seq_ends[None, :]).astype(jnp.int32), axis=1))
    owner_mask = seg_ids[:, None] == jnp.arange(lengths.shape[0], dtype=jnp.int32)[None, :]
    positions = row_index - lax.optimization_barrier(jnp.sum(jnp.where(owner_mask, starts[None, :], 0), axis=1)).astype(jnp.int32)
    return (seg_ids, positions)

def layer_norm(values, gain_vec, shift_vec):
    average = lax.optimization_barrier(jnp.mean(values, axis=-1, keepdims=True))
    centred = values - average
    spread = lax.optimization_barrier(jnp.mean(centred * centred, axis=-1, keepdims=True))
    return centred * lax.rsqrt(spread + 1e-05) * gain_vec + shift_vec

def rotary_tables(positions, head_dim):
    rot_dims = head_dim // 4
    half_rot = rot_dims // 2
    inv_freq = 10000.0 ** (-(jnp.arange(half_rot, dtype=jnp.float32) * 2.0 / rot_dims))
    angles = positions.astype(jnp.float32)[:, None] * inv_freq[None, :]
    angles = jnp.concatenate([angles, angles], axis=-1)
    return (jnp.cos(angles), jnp.sin(angles))

def rotate(vectors, cosine_table, sine_table):
    rot_dims = cosine_table.shape[-1]
    half_rot = rot_dims // 2
    rot_part = vectors[..., :rot_dims]
    turned = jnp.concatenate([-rot_part[..., half_rot:], rot_part[..., :half_rot]], axis=-1)
    result = rot_part * cosine_table[:, None, :] + turned * sine_table[:, None, :]
    return jnp.concatenate([result, vectors[..., rot_dims:]], axis=-1)

def attention(query_low, key_low, value_low, seg_ids):
    highest = lax.Precision.HIGHEST
    group_rows = query_low.shape[0]
    block_rows = min(512, group_rows)
    block_count = group_rows // block_rows
    key_index = jnp.arange(group_rows, dtype=jnp.int32)
    score_scale = HD ** (-0.5)

    def block_fn(number):
        begin_row = (number * block_rows).astype(jnp.int32)
        query_blk = lax.dynamic_slice_in_dim(query_low, begin_row, block_rows, 0)
        seg_blk = lax.dynamic_slice_in_dim(seg_ids, begin_row, block_rows, 0)
        query_index = begin_row + jnp.arange(block_rows, dtype=jnp.int32)
        scores = low_back(jnp.einsum('qhd,khd->hqk', query_blk, key_low, precision=highest) * score_scale)
        allowed = (key_index[None, :] <= query_index[:, None]) & (seg_ids[None, :] == seg_blk[:, None])
        scores = jnp.where(allowed[None], scores, -1e+30)
        probs = jax.nn.softmax(scores, axis=-1)
        return jnp.einsum('hqk,khd->qhd', low(probs), value_low, precision=highest)
    stacked = lax.map(jax.checkpoint(block_fn), jnp.arange(block_count, dtype=jnp.int32))
    return stacked.reshape(group_rows, query_low.shape[1], query_low.shape[2])

def group_layer(group_x, seg_ids, positions, params):
    attn_gain, attn_shift, mlp_gain, mlp_shift, qkv_weight, qkv_bias, dense_weight, dense_bias, fc_weight, fc_bias, proj_weight, proj_bias = params
    highest = lax.Precision.HIGHEST
    normed_attn = low(layer_norm(group_x, attn_gain, attn_shift))
    normed_mlp = low(layer_norm(group_x, mlp_gain, mlp_shift))
    merged_lin = low_back(jnp.dot(normed_attn, qkv_weight.reshape(D, 3 * H * HD), precision=highest) + qkv_bias)
    merged_lin = merged_lin.reshape(GRP, H, 3 * HD)
    cosine_table, sine_table = rotary_tables(positions, HD)
    query_low = low(rotate(merged_lin[..., :HD], cosine_table, sine_table))
    key_low = low(rotate(merged_lin[..., HD:2 * HD], cosine_table, sine_table))
    value_low = low(merged_lin[..., 2 * HD:])
    heads_out = low(low_back(attention(query_low, key_low, value_low, seg_ids)))
    attn_part = jnp.dot(heads_out.reshape(GRP, H * HD), dense_weight.reshape(D, H * HD).T, precision=highest)
    fc_pre = low_back(jnp.dot(normed_mlp, fc_weight, precision=highest) + fc_bias)
    act_low = low(jax.nn.gelu(fc_pre, approximate=False))
    mlp_part = jnp.dot(act_low, proj_weight.T, precision=highest)
    return group_x + attn_part + mlp_part + dense_bias + proj_bias

def reference(hidden_in, out_grad, seq_lengths, attn_gain, attn_shift, mlp_gain, mlp_shift, qkv_weight, qkv_bias, dense_weight, dense_bias, fc_weight, fc_bias, proj_weight, proj_bias):
    params = tuple((item.astype(jnp.float32) for item in (attn_gain, attn_shift, mlp_gain, mlp_shift, qkv_weight, qkv_bias, dense_weight, dense_bias, fc_weight, fc_bias, proj_weight, proj_bias)))
    seg_all, pos_all = jax.vmap(lambda lengths: layout(lengths, GRP))(seq_lengths)

    def forward(x_all, param_set):
        groups = x_all.reshape(N_DP, GRP, D)

        def scan_step(carry_in, inputs):
            group_x, seg_ids, positions = inputs
            return (carry_in, group_layer(group_x, seg_ids, positions, param_set))
        _, stacked = lax.scan(scan_step, jnp.zeros((), jnp.float32), (groups, seg_all, pos_all))
        return stacked.reshape(TOKENS, D)
    block_out, pullback = jax.vjp(forward, hidden_in.astype(jnp.float32), params)
    input_grad, param_grads = pullback(out_grad.astype(jnp.float32))
    g_attn_gain, g_attn_shift, g_mlp_gain, g_mlp_shift, g_qkv_weight, g_qkv_bias, g_dense_weight, g_dense_bias, g_fc_weight, g_fc_bias, g_proj_weight, g_proj_bias = param_grads
    return (block_out.astype(jnp.bfloat16), input_grad, g_attn_gain, g_attn_shift, g_mlp_gain, g_mlp_shift, g_qkv_weight, g_qkv_bias, g_dense_weight, g_dense_bias, g_fc_weight, g_fc_bias, g_proj_weight, g_proj_bias)
```

```python
import jax
import jax.numpy as jnp
from jax import lax
from jax.sharding import PartitionSpec as P


def layout(lengths, group_rows):
    seq_index = jnp.arange(lengths.shape[0], dtype=jnp.int32)
    seq_ends = jnp.sum(
        jnp.where(seq_index[None, :] <= seq_index[:, None], lengths[None, :], 0), axis=1
    )
    starts = seq_ends - lengths
    row_index = jnp.arange(group_rows, dtype=jnp.int32)
    seg_ids = jnp.sum((row_index[:, None] >= seq_ends[None, :]).astype(jnp.int32), axis=1)
    owner_mask = seg_ids[:, None] == jnp.arange(lengths.shape[0], dtype=jnp.int32)[None, :]
    positions = row_index - jnp.sum(jnp.where(owner_mask, starts[None, :], 0), axis=1)
    return (seg_ids, positions)


def layer_norm(values, gain_vec, shift_vec):
    average = jnp.mean(values, axis=-1, keepdims=True)
    centred = values - average
    spread = jnp.mean(centred * centred, axis=-1, keepdims=True)
    return centred * lax.rsqrt(spread + 1e-05) * gain_vec + shift_vec


def rotary_tables(positions, head_dim):
    rot_dims = head_dim // 4
    half_rot = rot_dims // 2
    inv_freq = 10000.0 ** (-(jnp.arange(half_rot, dtype=jnp.float32) * 2.0 / rot_dims))
    angles = positions.astype(jnp.float32)[:, None] * inv_freq[None, :]
    angles = jnp.concatenate([angles, angles], axis=-1)
    return (jnp.cos(angles), jnp.sin(angles))


def rotate(vectors, cosine_table, sine_table):
    rot_dims = cosine_table.shape[-1]
    half_rot = rot_dims // 2
    rot_part = vectors[..., :rot_dims]
    turned = jnp.concatenate([-rot_part[..., half_rot:], rot_part[..., :half_rot]], axis=-1)
    result = rot_part * cosine_table[:, None, :] + turned * sine_table[:, None, :]
    return jnp.concatenate([result, vectors[..., rot_dims:]], axis=-1)


def exact_gelu(values):
    return jax.nn.gelu(values, approximate=False)


def body(
    hidden_in,
    out_grad,
    seq_lengths,
    attn_gain,
    attn_shift,
    mlp_gain,
    mlp_shift,
    qkv_weight,
    qkv_bias,
    dense_weight,
    dense_bias,
    fc_weight,
    fc_bias,
    proj_weight,
    proj_bias,
):
    tensor_index = lax.axis_index("tensor")
    tensor_count = lax.axis_size("tensor")
    local_rows = hidden_in.shape[0]
    group_rows = local_rows * tensor_count
    gathered = (
        lax.all_gather(qkv_weight, "dp", axis=0, tiled=True),
        lax.all_gather(dense_weight, "dp", axis=0, tiled=True),
        lax.all_gather(fc_weight, "dp", axis=0, tiled=True),
        lax.all_gather(proj_weight, "dp", axis=0, tiled=True),
        lax.all_gather(attn_gain, "dp", axis=0, tiled=True),
        lax.all_gather(attn_shift, "dp", axis=0, tiled=True),
        lax.all_gather(mlp_gain, "dp", axis=0, tiled=True),
        lax.all_gather(mlp_shift, "dp", axis=0, tiled=True),
        lax.all_gather(qkv_bias, "dp", axis=0, tiled=True),
        lax.all_gather(dense_bias, "dp", axis=0, tiled=True),
        lax.all_gather(fc_bias, "dp", axis=0, tiled=True),
        lax.all_gather(proj_bias, "dp", axis=0, tiled=True),
    )
    (
        w_qkv,
        w_dense,
        w_fc,
        w_proj,
        gain_attn,
        shift_attn,
        gain_mlp,
        shift_mlp,
        bias_qkv,
        bias_dense,
        bias_fc,
        bias_proj,
    ) = gathered
    model_width = w_qkv.shape[0]
    head_count = w_qkv.shape[1]
    triple_width = w_qkv.shape[2]
    head_dim = w_dense.shape[2]
    hidden_units = w_fc.shape[1]
    qkv_cols = head_count * triple_width
    attn_cols = head_count * head_dim
    my_bias_qkv = lax.dynamic_slice_in_dim(bias_qkv, tensor_index * qkv_cols, qkv_cols).astype(
        jnp.float32
    )
    my_bias_fc = lax.dynamic_slice_in_dim(
        bias_fc, tensor_index * hidden_units, hidden_units
    ).astype(jnp.float32)
    gain_attn_f = gain_attn.astype(jnp.float32)
    shift_attn_f = shift_attn.astype(jnp.float32)
    gain_mlp_f = gain_mlp.astype(jnp.float32)
    shift_mlp_f = shift_mlp.astype(jnp.float32)
    seg_ids, positions = layout(seq_lengths[0], group_rows)
    x_rows = hidden_in.astype(jnp.float32)

    def norms(values, gain_one, shift_one, gain_two, shift_two):
        return (layer_norm(values, gain_one, shift_one), layer_norm(values, gain_two, shift_two))

    (normed_one, normed_two), norm_back = jax.vjp(
        norms, x_rows, gain_attn_f, shift_attn_f, gain_mlp_f, shift_mlp_f
    )
    normed_attn, normed_mlp = (
        lax.all_gather(normed_one.astype(jnp.bfloat16), "tensor", axis=0, tiled=True),
        lax.all_gather(normed_two.astype(jnp.bfloat16), "tensor", axis=0, tiled=True),
    )
    merged_lin = (
        jnp.dot(
            normed_attn, w_qkv.reshape(model_width, qkv_cols), preferred_element_type=jnp.float32
        )
        + my_bias_qkv
    )
    merged_lin = merged_lin.reshape(group_rows, head_count, triple_width)
    cosine_table, sine_table = rotary_tables(positions, head_dim)

    def turn_pair(query_lin, key_lin):
        return (
            rotate(query_lin, cosine_table, sine_table),
            rotate(key_lin, cosine_table, sine_table),
        )

    (query_rot, key_rot), turn_back = jax.vjp(
        turn_pair, merged_lin[..., :head_dim], merged_lin[..., head_dim : 2 * head_dim]
    )
    query_low = query_rot.astype(jnp.bfloat16)
    key_low = key_rot.astype(jnp.bfloat16)
    value_low = merged_lin[..., 2 * head_dim :].astype(jnp.bfloat16)
    score_scale = head_dim ** (-0.5)
    block_rows = min(512, group_rows)
    block_count = group_rows // block_rows
    row_index = jnp.arange(group_rows, dtype=jnp.int32)

    def masked_scores(number):
        begin_row = number * block_rows
        end_row = begin_row + block_rows
        scores = (
            jnp.einsum(
                "qhd,khd->hqk",
                query_low[begin_row:end_row],
                key_low[:end_row],
                preferred_element_type=jnp.float32,
            )
            * score_scale
        )
        allowed = (row_index[None, :end_row] <= row_index[begin_row:end_row, None]) & (
            seg_ids[None, :end_row] == seg_ids[begin_row:end_row, None]
        )
        return jnp.where(allowed[None], scores, -1e30)

    head_blocks = []
    log_totals = []
    for number in range(block_count):
        end_row = (number + 1) * block_rows
        scores = masked_scores(number)
        peak_score = jnp.max(scores, axis=-1, keepdims=True)
        weights = jnp.exp(scores - peak_score)
        norm_total = jnp.sum(weights, axis=-1, keepdims=True)
        log_totals.append(peak_score + jnp.log(norm_total))
        prob_low = (weights / norm_total).astype(jnp.bfloat16)
        head_blocks.append(
            jnp.einsum(
                "hqk,khd->qhd", prob_low, value_low[:end_row], preferred_element_type=jnp.float32
            )
        )
    heads_flat = (
        jnp.concatenate(head_blocks, axis=0).astype(jnp.bfloat16).reshape(group_rows, attn_cols)
    )
    attn_part = jnp.einsum(
        "gc,dc->gd",
        heads_flat,
        w_dense.reshape(model_width, attn_cols),
        preferred_element_type=jnp.float32,
    )
    fc_pre = jnp.dot(normed_mlp, w_fc, preferred_element_type=jnp.float32) + my_bias_fc
    act_full, gelu_back = jax.vjp(exact_gelu, fc_pre)
    act_low = act_full.astype(jnp.bfloat16)
    mlp_part = jnp.einsum("gf,df->gd", act_low, w_proj, preferred_element_type=jnp.float32)
    branch_rows = lax.psum_scatter(
        (attn_part + mlp_part).astype(jnp.bfloat16), "tensor", scatter_dimension=0, tiled=True
    ).astype(jnp.float32)
    block_out = (
        x_rows + branch_rows + bias_dense.astype(jnp.float32) + bias_proj.astype(jnp.float32)
    ).astype(jnp.bfloat16)
    w_qkv, w_dense, w_fc, w_proj = (
        lax.all_gather(qkv_weight, "dp", axis=0, tiled=True),
        lax.all_gather(dense_weight, "dp", axis=0, tiled=True),
        lax.all_gather(fc_weight, "dp", axis=0, tiled=True),
        lax.all_gather(proj_weight, "dp", axis=0, tiled=True),
    )
    cot_all = lax.all_gather(out_grad, "tensor", axis=0, tiled=True)
    grad_act = jnp.dot(cot_all, w_proj, preferred_element_type=jnp.float32)
    grad_proj = jnp.einsum("gd,gf->df", cot_all, act_low, preferred_element_type=jnp.float32)
    grad_pre = gelu_back(grad_act)[0].astype(jnp.bfloat16)
    grad_fc = jnp.einsum("gd,gf->df", normed_mlp, grad_pre, preferred_element_type=jnp.float32)
    fc_bias_part = jnp.sum(grad_pre, axis=0, dtype=jnp.float32)
    grad_normed_mlp = jnp.einsum("gf,df->gd", grad_pre, w_fc, preferred_element_type=jnp.float32)
    dense_flat = w_dense.reshape(model_width, attn_cols)
    grad_heads = (
        jnp.dot(cot_all, dense_flat, preferred_element_type=jnp.float32)
        .astype(jnp.bfloat16)
        .reshape(group_rows, head_count, head_dim)
    )
    grad_dense = jnp.einsum(
        "gd,gc->dc", cot_all, heads_flat, preferred_element_type=jnp.float32
    ).reshape(model_width, head_count, head_dim)
    query_grads = []
    grad_key = jnp.zeros((group_rows, head_count, head_dim), jnp.float32)
    grad_value = jnp.zeros((group_rows, head_count, head_dim), jnp.float32)
    for number in range(block_count):
        begin_row = number * block_rows
        end_row = begin_row + block_rows
        probs = jnp.exp(masked_scores(number) - log_totals[number])
        heads_blk = grad_heads[begin_row:end_row]
        grad_probs = jnp.einsum(
            "qhd,khd->hqk", heads_blk, value_low[:end_row], preferred_element_type=jnp.float32
        )
        row_delta = jnp.sum(probs * grad_probs, axis=-1, keepdims=True)
        grad_scores = (probs * (grad_probs - row_delta)).astype(jnp.bfloat16)
        query_grads.append(
            jnp.einsum(
                "hqk,khd->qhd", grad_scores, key_low[:end_row], preferred_element_type=jnp.float32
            )
            * score_scale
        )
        grad_key = grad_key.at[:end_row].add(
            jnp.einsum(
                "hqk,qhd->khd",
                grad_scores,
                query_low[begin_row:end_row],
                preferred_element_type=jnp.float32,
            )
            * score_scale
        )
        grad_value = grad_value.at[:end_row].add(
            jnp.einsum(
                "hqk,qhd->khd",
                probs.astype(jnp.bfloat16),
                heads_blk,
                preferred_element_type=jnp.float32,
            )
        )
    grad_query = jnp.concatenate(query_grads, axis=0)
    grad_query_lin, grad_key_lin = turn_back((grad_query, grad_key))
    grad_merged = (
        jnp.concatenate([grad_query_lin, grad_key_lin, grad_value], axis=-1)
        .astype(jnp.bfloat16)
        .reshape(group_rows, qkv_cols)
    )
    grad_qkv = jnp.einsum(
        "gd,gc->dc", normed_attn, grad_merged, preferred_element_type=jnp.float32
    ).reshape(model_width, head_count, triple_width)
    qkv_bias_part = jnp.sum(grad_merged, axis=0, dtype=jnp.float32)
    grad_normed_attn = jnp.einsum(
        "gc,dc->gd",
        grad_merged,
        w_qkv.reshape(model_width, qkv_cols),
        preferred_element_type=jnp.float32,
    )
    cot_rows = out_grad.astype(jnp.float32)
    local_attn, local_mlp = (
        lax.psum_scatter(
            grad_normed_attn.astype(jnp.bfloat16), "tensor", scatter_dimension=0, tiled=True
        ).astype(jnp.float32),
        lax.psum_scatter(
            grad_normed_mlp.astype(jnp.bfloat16), "tensor", scatter_dimension=0, tiled=True
        ).astype(jnp.float32),
    )
    grad_x, grad_gain_attn, grad_shift_attn, grad_gain_mlp, grad_shift_mlp = norm_back(
        (local_attn, local_mlp)
    )
    input_grad = cot_rows + grad_x
    cot_sums = jnp.sum(cot_rows, axis=0)
    full_qkv_bias = lax.dynamic_update_slice_in_dim(
        jnp.zeros((qkv_cols * tensor_count,), jnp.float32),
        qkv_bias_part,
        tensor_index * qkv_cols,
        0,
    )
    full_fc_bias = lax.dynamic_update_slice_in_dim(
        jnp.zeros((hidden_units * tensor_count,), jnp.float32),
        fc_bias_part,
        tensor_index * hidden_units,
        0,
    )
    small_sums = (
        lax.psum_scatter(grad_gain_attn, ("dp", "tensor"), scatter_dimension=0, tiled=True),
        lax.psum_scatter(grad_shift_attn, ("dp", "tensor"), scatter_dimension=0, tiled=True),
        lax.psum_scatter(grad_gain_mlp, ("dp", "tensor"), scatter_dimension=0, tiled=True),
        lax.psum_scatter(grad_shift_mlp, ("dp", "tensor"), scatter_dimension=0, tiled=True),
        lax.psum_scatter(full_qkv_bias, ("dp", "tensor"), scatter_dimension=0, tiled=True),
        lax.psum_scatter(cot_sums, ("dp", "tensor"), scatter_dimension=0, tiled=True),
        lax.psum_scatter(full_fc_bias, ("dp", "tensor"), scatter_dimension=0, tiled=True),
    )
    large_sums = (
        lax.psum_scatter(grad_qkv, "dp", scatter_dimension=0, tiled=True),
        lax.psum_scatter(grad_dense, "dp", scatter_dimension=0, tiled=True),
        lax.psum_scatter(grad_fc, "dp", scatter_dimension=0, tiled=True),
        lax.psum_scatter(grad_proj, "dp", scatter_dimension=0, tiled=True),
    )
    return (
        block_out,
        input_grad,
        small_sums[0],
        small_sums[1],
        small_sums[2],
        small_sums[3],
        large_sums[0],
        small_sums[4],
        large_sums[1],
        small_sums[5],
        large_sums[2],
        small_sums[6],
        large_sums[3],
        small_sums[5],
    )


def solution(mesh):
    in_specs = (
        P(("dp", "tensor"), None),
        P(("dp", "tensor"), None),
        P("dp", None),
        P("dp"),
        P("dp"),
        P("dp"),
        P("dp"),
        P("dp", "tensor", None),
        P("dp"),
        P("dp", "tensor", None),
        P("dp"),
        P("dp", "tensor"),
        P("dp"),
        P("dp", "tensor"),
        P("dp"),
    )
    out_specs = (
        P(("dp", "tensor"), None),
        P(("dp", "tensor"), None),
        P(("dp", "tensor")),
        P(("dp", "tensor")),
        P(("dp", "tensor")),
        P(("dp", "tensor")),
        P("dp", "tensor", None),
        P(("dp", "tensor")),
        P("dp", "tensor", None),
        P(("dp", "tensor")),
        P("dp", "tensor"),
        P(("dp", "tensor")),
        P("dp", "tensor"),
        P(("dp", "tensor")),
    )
    return jax.shard_map(body, mesh=mesh, in_specs=in_specs, out_specs=out_specs, check_vma=False)
```

```python
import jax
import jax.numpy as jnp
from jax import lax
from jax.sharding import PartitionSpec as P


def layout(lengths, group_rows):
    seq_index = jnp.arange(lengths.shape[0], dtype=jnp.int32)
    seq_ends = jnp.sum(
        jnp.where(seq_index[None, :] <= seq_index[:, None], lengths[None, :], 0), axis=1
    )
    starts = seq_ends - lengths
    row_index = jnp.arange(group_rows, dtype=jnp.int32)
    seg_ids = jnp.sum((row_index[:, None] >= seq_ends[None, :]).astype(jnp.int32), axis=1)
    owner_mask = seg_ids[:, None] == jnp.arange(lengths.shape[0], dtype=jnp.int32)[None, :]
    positions = row_index - jnp.sum(jnp.where(owner_mask, starts[None, :], 0), axis=1)
    return (seg_ids, positions)


def steps_from(size, turn):
    steps = []
    step = 1
    while step < size:
        steps.append(step)
        step *= 2
    return steps[turn:] + steps[:turn]


def exchange(values, axis, step):
    size = lax.axis_size(axis)
    return lax.ppermute(values, axis, [(i, i ^ step) for i in range(size)])


def gather_pairs(block, axis, turn=0):
    size = lax.axis_size(axis)
    index = lax.axis_index(axis)
    order = steps_from(size, turn)[::-1]
    held = block
    for step in order:
        other = exchange(held, axis, step)
        is_low = (index // step) % 2 == 0
        held = jnp.stack([jnp.where(is_low, held, other), jnp.where(is_low, other, held)])
    placed = order[::-1]
    want = sorted(placed, reverse=True)
    tail = range(len(order), held.ndim)
    held = held.transpose([placed.index(step) for step in want] + list(tail))
    return held.reshape((size * block.shape[0],) + block.shape[1:])


def scatter_pairs(full, axis, turn=0, sent=jnp.bfloat16):
    size = lax.axis_size(axis)
    index = lax.axis_index(axis)
    left = sorted(steps_from(size, 0), reverse=True)
    held = full.reshape([2] * len(left) + [full.shape[0] // size] + list(full.shape[1:]))
    for step in steps_from(size, turn):
        spot = left.index(step)
        bit = (index // step) % 2
        away = lax.dynamic_index_in_dim(held, 1 - bit, spot, keepdims=False).astype(sent)
        kept = lax.dynamic_index_in_dim(held, bit, spot, keepdims=False).astype(jnp.float32)
        held = kept + exchange(away, axis, step).astype(jnp.float32)
        left.remove(step)
    return held


def layer_norm(values, gain_vec, shift_vec):
    average = jnp.mean(values, axis=-1, keepdims=True)
    centred = values - average
    spread = jnp.mean(centred * centred, axis=-1, keepdims=True)
    return centred * lax.rsqrt(spread + 1e-05) * gain_vec + shift_vec


def rotary_tables(positions, head_dim):
    rot_dims = head_dim // 4
    half_rot = rot_dims // 2
    inv_freq = 10000.0 ** (-(jnp.arange(half_rot, dtype=jnp.float32) * 2.0 / rot_dims))
    angles = positions.astype(jnp.float32)[:, None] * inv_freq[None, :]
    angles = jnp.concatenate([angles, angles], axis=-1)
    return (jnp.cos(angles), jnp.sin(angles))


def rotate(vectors, cosine_table, sine_table):
    rot_dims = cosine_table.shape[-1]
    half_rot = rot_dims // 2
    rot_part = vectors[..., :rot_dims]
    turned = jnp.concatenate([-rot_part[..., half_rot:], rot_part[..., :half_rot]], axis=-1)
    result = rot_part * cosine_table[:, None, :] + turned * sine_table[:, None, :]
    return jnp.concatenate([result, vectors[..., rot_dims:]], axis=-1)


def exact_gelu(values):
    return jax.nn.gelu(values, approximate=False)


def body(
    hidden_in,
    out_grad,
    seq_lengths,
    attn_gain,
    attn_shift,
    mlp_gain,
    mlp_shift,
    qkv_weight,
    qkv_bias,
    dense_weight,
    dense_bias,
    fc_weight,
    fc_bias,
    proj_weight,
    proj_bias,
):
    tensor_index = lax.axis_index("tensor")
    tensor_count = lax.axis_size("tensor")
    local_rows = hidden_in.shape[0]
    group_rows = local_rows * tensor_count
    rows_all = gather_pairs(hidden_in, "tensor")
    cot_all = gather_pairs(out_grad, "tensor")
    smalls = (
        attn_gain,
        attn_shift,
        mlp_gain,
        mlp_shift,
        qkv_bias,
        dense_bias,
        fc_bias,
        proj_bias,
    )
    packed = gather_pairs(jnp.concatenate(smalls)[None], "dp", 0)
    parts = []
    begin = 0
    for item in smalls:
        parts.append(packed[:, begin : begin + item.shape[0]].reshape(-1))
        begin += item.shape[0]
    (
        gain_attn,
        shift_attn,
        gain_mlp,
        shift_mlp,
        bias_qkv,
        bias_dense,
        bias_fc,
        bias_proj,
    ) = parts
    head_count, triple_width = qkv_weight.shape[1:]
    w_qkv = gather_pairs(qkv_weight.reshape(qkv_weight.shape[0], -1), "dp", 2)
    w_dense = gather_pairs(dense_weight.reshape(dense_weight.shape[0], -1), "dp", 2)
    w_fc = gather_pairs(fc_weight, "dp", 0)
    w_proj = gather_pairs(proj_weight, "dp", 1)
    model_width = w_qkv.shape[0]
    head_dim = dense_weight.shape[2]
    hidden_units = w_fc.shape[1]
    qkv_cols = head_count * triple_width
    attn_cols = head_count * head_dim
    my_bias_qkv = lax.dynamic_slice_in_dim(bias_qkv, tensor_index * qkv_cols, qkv_cols).astype(
        jnp.float32
    )
    my_bias_fc = lax.dynamic_slice_in_dim(
        bias_fc, tensor_index * hidden_units, hidden_units
    ).astype(jnp.float32)
    gain_attn_f = gain_attn.astype(jnp.float32)
    shift_attn_f = shift_attn.astype(jnp.float32)
    gain_mlp_f = gain_mlp.astype(jnp.float32)
    shift_mlp_f = shift_mlp.astype(jnp.float32)
    seg_ids, positions = layout(seq_lengths[0], group_rows)
    x_rows = hidden_in.astype(jnp.float32)

    def norms(values, gain_one, shift_one, gain_two, shift_two):
        return (layer_norm(values, gain_one, shift_one), layer_norm(values, gain_two, shift_two))

    _, norm_back = jax.vjp(
        norms, x_rows, gain_attn_f, shift_attn_f, gain_mlp_f, shift_mlp_f
    )
    normed_attn, normed_mlp = (
        normed.astype(jnp.bfloat16)
        for normed in norms(
            rows_all.astype(jnp.float32), gain_attn_f, shift_attn_f, gain_mlp_f, shift_mlp_f
        )
    )
    merged_lin = (
        jnp.dot(
            normed_attn, w_qkv, preferred_element_type=jnp.float32
        )
        + my_bias_qkv
    )
    merged_lin = merged_lin.reshape(group_rows, head_count, triple_width)
    cosine_table, sine_table = rotary_tables(positions, head_dim)

    def turn_pair(query_lin, key_lin):
        return (
            rotate(query_lin, cosine_table, sine_table),
            rotate(key_lin, cosine_table, sine_table),
        )

    (query_rot, key_rot), turn_back = jax.vjp(
        turn_pair, merged_lin[..., :head_dim], merged_lin[..., head_dim : 2 * head_dim]
    )
    query_low = query_rot.astype(jnp.bfloat16)
    key_low = key_rot.astype(jnp.bfloat16)
    value_low = merged_lin[..., 2 * head_dim :].astype(jnp.bfloat16)
    score_scale = head_dim ** (-0.5)
    block_rows = min(512, group_rows)
    block_count = group_rows // block_rows
    row_index = jnp.arange(group_rows, dtype=jnp.int32)

    def masked_scores(number):
        begin_row = number * block_rows
        end_row = begin_row + block_rows
        scores = (
            jnp.einsum(
                "qhd,khd->hqk",
                query_low[begin_row:end_row],
                key_low[:end_row],
                preferred_element_type=jnp.float32,
            )
            * score_scale
        )
        allowed = (row_index[None, :end_row] <= row_index[begin_row:end_row, None]) & (
            seg_ids[None, :end_row] == seg_ids[begin_row:end_row, None]
        )
        return jnp.where(allowed[None], scores, -1e30)

    head_blocks = []
    log_totals = []
    for number in range(block_count):
        end_row = (number + 1) * block_rows
        scores = masked_scores(number)
        peak_score = jnp.max(scores, axis=-1, keepdims=True)
        weights = jnp.exp(scores - peak_score)
        norm_total = jnp.sum(weights, axis=-1, keepdims=True)
        log_totals.append(peak_score + jnp.log(norm_total))
        prob_low = (weights / norm_total).astype(jnp.bfloat16)
        head_blocks.append(
            jnp.einsum(
                "hqk,khd->qhd", prob_low, value_low[:end_row], preferred_element_type=jnp.float32
            )
        )
    heads_flat = (
        jnp.concatenate(head_blocks, axis=0).astype(jnp.bfloat16).reshape(group_rows, attn_cols)
    )
    attn_part = jnp.einsum(
        "gc,dc->gd",
        heads_flat,
        w_dense,
        preferred_element_type=jnp.float32,
    )
    fc_pre = jnp.dot(normed_mlp, w_fc, preferred_element_type=jnp.float32) + my_bias_fc
    act_full, gelu_back = jax.vjp(exact_gelu, fc_pre)
    act_low = act_full.astype(jnp.bfloat16)
    mlp_part = jnp.einsum("gf,df->gd", act_low, w_proj, preferred_element_type=jnp.float32)
    branch_rows = scatter_pairs(attn_part + mlp_part, "tensor")
    block_out = (
        x_rows + branch_rows + bias_dense.astype(jnp.float32) + bias_proj.astype(jnp.float32)
    ).astype(jnp.bfloat16)
    grad_act = jnp.dot(cot_all, w_proj, preferred_element_type=jnp.float32)
    grad_proj = jnp.einsum("gd,gf->df", cot_all, act_low, preferred_element_type=jnp.float32)
    grad_pre = gelu_back(grad_act)[0].astype(jnp.bfloat16)
    grad_fc = jnp.einsum("gd,gf->df", normed_mlp, grad_pre, preferred_element_type=jnp.float32)
    fc_bias_part = jnp.sum(grad_pre, axis=0, dtype=jnp.float32)
    grad_normed_mlp = jnp.einsum("gf,df->gd", grad_pre, w_fc, preferred_element_type=jnp.float32)
    grad_heads = (
        jnp.dot(cot_all, w_dense, preferred_element_type=jnp.float32)
        .astype(jnp.bfloat16)
        .reshape(group_rows, head_count, head_dim)
    )
    grad_dense = jnp.einsum(
        "gd,gc->dc", cot_all, heads_flat, preferred_element_type=jnp.float32
    )
    query_grads = []
    grad_key = jnp.zeros((group_rows, head_count, head_dim), jnp.float32)
    grad_value = jnp.zeros((group_rows, head_count, head_dim), jnp.float32)
    for number in range(block_count):
        begin_row = number * block_rows
        end_row = begin_row + block_rows
        probs = jnp.exp(masked_scores(number) - log_totals[number])
        heads_blk = grad_heads[begin_row:end_row]
        grad_probs = jnp.einsum(
            "qhd,khd->hqk", heads_blk, value_low[:end_row], preferred_element_type=jnp.float32
        )
        row_delta = jnp.sum(probs * grad_probs, axis=-1, keepdims=True)
        grad_scores = (probs * (grad_probs - row_delta)).astype(jnp.bfloat16)
        query_grads.append(
            jnp.einsum(
                "hqk,khd->qhd", grad_scores, key_low[:end_row], preferred_element_type=jnp.float32
            )
            * score_scale
        )
        grad_key = grad_key.at[:end_row].add(
            jnp.einsum(
                "hqk,qhd->khd",
                grad_scores,
                query_low[begin_row:end_row],
                preferred_element_type=jnp.float32,
            )
            * score_scale
        )
        grad_value = grad_value.at[:end_row].add(
            jnp.einsum(
                "hqk,qhd->khd",
                probs.astype(jnp.bfloat16),
                heads_blk,
                preferred_element_type=jnp.float32,
            )
        )
    grad_query = jnp.concatenate(query_grads, axis=0)
    grad_query_lin, grad_key_lin = turn_back((grad_query, grad_key))
    grad_merged = (
        jnp.concatenate([grad_query_lin, grad_key_lin, grad_value], axis=-1)
        .astype(jnp.bfloat16)
        .reshape(group_rows, qkv_cols)
    )
    grad_qkv = jnp.einsum(
        "gd,gc->dc", normed_attn, grad_merged, preferred_element_type=jnp.float32
    )
    qkv_bias_part = jnp.sum(grad_merged, axis=0, dtype=jnp.float32)
    grad_normed_attn = jnp.einsum(
        "gc,dc->gd",
        grad_merged,
        w_qkv,
        preferred_element_type=jnp.float32,
    )
    cot_rows = out_grad.astype(jnp.float32)
    local_attn, local_mlp = (
        scatter_pairs(grad_normed_attn, "tensor"),
        scatter_pairs(grad_normed_mlp, "tensor"),
    )
    grad_x, grad_gain_attn, grad_shift_attn, grad_gain_mlp, grad_shift_mlp = norm_back(
        (local_attn, local_mlp)
    )
    input_grad = cot_rows + grad_x
    cot_sums = jnp.sum(cot_rows, axis=0)
    full_qkv_bias = lax.dynamic_update_slice_in_dim(
        jnp.zeros((qkv_cols * tensor_count,), jnp.float32),
        qkv_bias_part,
        tensor_index * qkv_cols,
        0,
    )
    full_fc_bias = lax.dynamic_update_slice_in_dim(
        jnp.zeros((hidden_units * tensor_count,), jnp.float32),
        fc_bias_part,
        tensor_index * hidden_units,
        0,
    )
    owners = lax.axis_size("dp") * tensor_count
    small_list = (
        grad_gain_attn,
        grad_shift_attn,
        grad_gain_mlp,
        grad_shift_mlp,
        full_qkv_bias,
        cot_sums,
        full_fc_bias,
    )
    small_packed = jnp.concatenate([item.reshape(owners, -1) for item in small_list], axis=1)
    small_packed = scatter_pairs(small_packed, "dp", 0, jnp.float32)
    small_packed = scatter_pairs(small_packed, "tensor", 0, jnp.float32).reshape(-1)
    small_sums = []
    begin = 0
    for item in small_list:
        count = item.shape[0] // owners
        small_sums.append(small_packed[begin : begin + count])
        begin += count
    third = qkv_cols // 3
    sum_qkv = jnp.concatenate(
        [
            scatter_pairs(grad_qkv[:, turn * third : (turn + 1) * third], "dp", turn)
            for turn in range(3)
        ],
        axis=1,
    )
    large_sums = (
        sum_qkv.reshape(qkv_weight.shape),
        scatter_pairs(grad_dense, "dp", 2).reshape(dense_weight.shape),
        scatter_pairs(grad_fc, "dp", 1),
        scatter_pairs(grad_proj, "dp", 2),
    )
    return (
        block_out,
        input_grad,
        small_sums[0],
        small_sums[1],
        small_sums[2],
        small_sums[3],
        large_sums[0],
        small_sums[4],
        large_sums[1],
        small_sums[5],
        large_sums[2],
        small_sums[6],
        large_sums[3],
        small_sums[5],
    )


def solution(mesh):
    in_specs = (
        P(("dp", "tensor"), None),
        P(("dp", "tensor"), None),
        P("dp", None),
        P("dp"),
        P("dp"),
        P("dp"),
        P("dp"),
        P("dp", "tensor", None),
        P("dp"),
        P("dp", "tensor", None),
        P("dp"),
        P("dp", "tensor"),
        P("dp"),
        P("dp", "tensor"),
        P("dp"),
    )
    out_specs = (
        P(("dp", "tensor"), None),
        P(("dp", "tensor"), None),
        P(("dp", "tensor")),
        P(("dp", "tensor")),
        P(("dp", "tensor")),
        P(("dp", "tensor")),
        P("dp", "tensor", None),
        P(("dp", "tensor")),
        P("dp", "tensor", None),
        P(("dp", "tensor")),
        P("dp", "tensor"),
        P(("dp", "tensor")),
        P("dp", "tensor"),
        P(("dp", "tensor")),
    )
    return jax.shard_map(body, mesh=mesh, in_specs=in_specs, out_specs=out_specs, check_vma=False)
```

```python
import jax
import jax.numpy as jnp
from jax import lax
from jax.sharding import PartitionSpec as P


def layout(lengths, group_rows):
    seq_index = jnp.arange(lengths.shape[0], dtype=jnp.int32)
    seq_ends = jnp.sum(
        jnp.where(seq_index[None, :] <= seq_index[:, None], lengths[None, :], 0), axis=1
    )
    starts = seq_ends - lengths
    row_index = jnp.arange(group_rows, dtype=jnp.int32)
    seg_ids = jnp.sum((row_index[:, None] >= seq_ends[None, :]).astype(jnp.int32), axis=1)
    owner_mask = seg_ids[:, None] == jnp.arange(lengths.shape[0], dtype=jnp.int32)[None, :]
    positions = row_index - jnp.sum(jnp.where(owner_mask, starts[None, :], 0), axis=1)
    return (seg_ids, positions)


def steps_from(size, turn):
    steps = []
    step = 1
    while step < size:
        steps.append(step)
        step *= 2
    return steps[turn:] + steps[:turn]


def exchange(values, axis, step):
    size = lax.axis_size(axis)
    return lax.ppermute(values, axis, [(i, i ^ step) for i in range(size)])


def gather_pairs(block, axis, turn=0):
    size = lax.axis_size(axis)
    index = lax.axis_index(axis)
    order = steps_from(size, turn)[::-1]
    held = block
    for step in order:
        other = exchange(held, axis, step)
        is_low = (index // step) % 2 == 0
        held = jnp.stack([jnp.where(is_low, held, other), jnp.where(is_low, other, held)])
    placed = order[::-1]
    want = sorted(placed, reverse=True)
    tail = range(len(order), held.ndim)
    held = held.transpose([placed.index(step) for step in want] + list(tail))
    return held.reshape((size * block.shape[0],) + block.shape[1:])


def scatter_pairs(full, axis, turn=0, sent=jnp.bfloat16):
    size = lax.axis_size(axis)
    index = lax.axis_index(axis)
    left = sorted(steps_from(size, 0), reverse=True)
    held = full.reshape([2] * len(left) + [full.shape[0] // size] + list(full.shape[1:]))
    for step in steps_from(size, turn):
        spot = left.index(step)
        bit = (index // step) % 2
        away = lax.dynamic_index_in_dim(held, 1 - bit, spot, keepdims=False).astype(sent)
        kept = lax.dynamic_index_in_dim(held, bit, spot, keepdims=False).astype(jnp.float32)
        held = kept + exchange(away, axis, step).astype(jnp.float32)
        left.remove(step)
    return held


def layer_norm(values, gain_vec, shift_vec):
    average = jnp.mean(values, axis=-1, keepdims=True)
    centred = values - average
    spread = jnp.mean(centred * centred, axis=-1, keepdims=True)
    return centred * lax.rsqrt(spread + 1e-05) * gain_vec + shift_vec


def rotary_tables(positions, head_dim):
    rot_dims = head_dim // 4
    half_rot = rot_dims // 2
    inv_freq = 10000.0 ** (-(jnp.arange(half_rot, dtype=jnp.float32) * 2.0 / rot_dims))
    angles = positions.astype(jnp.float32)[:, None] * inv_freq[None, :]
    angles = jnp.concatenate([angles, angles], axis=-1)
    return (jnp.cos(angles), jnp.sin(angles))


def rotate(vectors, cosine_table, sine_table):
    rot_dims = cosine_table.shape[-1]
    half_rot = rot_dims // 2
    rot_part = vectors[..., :rot_dims]
    turned = jnp.concatenate([-rot_part[..., half_rot:], rot_part[..., :half_rot]], axis=-1)
    result = rot_part * cosine_table[:, None, :] + turned * sine_table[:, None, :]
    return jnp.concatenate([result, vectors[..., rot_dims:]], axis=-1)


def exact_gelu(values):
    return jax.nn.gelu(values, approximate=False)


def body(
    hidden_in,
    out_grad,
    seq_lengths,
    attn_gain,
    attn_shift,
    mlp_gain,
    mlp_shift,
    qkv_weight,
    qkv_bias,
    dense_weight,
    dense_bias,
    fc_weight,
    fc_bias,
    proj_weight,
    proj_bias,
):
    tensor_index = lax.axis_index("tensor")
    tensor_count = lax.axis_size("tensor")
    local_rows = hidden_in.shape[0]
    group_rows = local_rows * tensor_count
    rows_all = gather_pairs(hidden_in, "tensor")
    cot_all = gather_pairs(out_grad, "tensor")
    smalls = (
        attn_gain,
        attn_shift,
        mlp_gain,
        mlp_shift,
        qkv_bias,
        dense_bias,
        fc_bias,
        proj_bias,
    )
    packed = gather_pairs(jnp.concatenate(smalls)[None], "dp", 0)
    parts = []
    begin = 0
    for item in smalls:
        parts.append(packed[:, begin : begin + item.shape[0]].reshape(-1))
        begin += item.shape[0]
    (
        gain_attn,
        shift_attn,
        gain_mlp,
        shift_mlp,
        bias_qkv,
        bias_dense,
        bias_fc,
        bias_proj,
    ) = parts
    head_count, triple_width = qkv_weight.shape[1:]
    w_qkv = gather_pairs(qkv_weight.reshape(qkv_weight.shape[0], -1), "dp", 2)
    w_dense = gather_pairs(dense_weight.reshape(dense_weight.shape[0], -1), "dp", 2)
    w_fc = gather_pairs(fc_weight, "dp", 0)
    w_proj = gather_pairs(proj_weight, "dp", 1)
    model_width = w_qkv.shape[0]
    head_dim = dense_weight.shape[2]
    hidden_units = w_fc.shape[1]
    qkv_cols = head_count * triple_width
    attn_cols = head_count * head_dim
    my_bias_qkv = lax.dynamic_slice_in_dim(bias_qkv, tensor_index * qkv_cols, qkv_cols).astype(
        jnp.float32
    )
    my_bias_fc = lax.dynamic_slice_in_dim(
        bias_fc, tensor_index * hidden_units, hidden_units
    ).astype(jnp.float32)
    gain_attn_f = gain_attn.astype(jnp.float32)
    shift_attn_f = shift_attn.astype(jnp.float32)
    gain_mlp_f = gain_mlp.astype(jnp.float32)
    shift_mlp_f = shift_mlp.astype(jnp.float32)
    seg_ids, positions = layout(seq_lengths[0], group_rows)
    x_rows = hidden_in.astype(jnp.float32)

    def norms(values, gain_one, shift_one, gain_two, shift_two):
        return (layer_norm(values, gain_one, shift_one), layer_norm(values, gain_two, shift_two))

    _, norm_back = jax.vjp(
        norms, x_rows, gain_attn_f, shift_attn_f, gain_mlp_f, shift_mlp_f
    )
    normed_attn, normed_mlp = (
        normed.astype(jnp.bfloat16)
        for normed in norms(
            rows_all.astype(jnp.float32), gain_attn_f, shift_attn_f, gain_mlp_f, shift_mlp_f
        )
    )
    merged_lin = (
        jnp.dot(
            normed_attn, w_qkv, preferred_element_type=jnp.float32
        )
        + my_bias_qkv
    )
    merged_lin = merged_lin.reshape(group_rows, head_count, triple_width)
    cosine_table, sine_table = rotary_tables(positions, head_dim)

    def turn_pair(query_lin, key_lin):
        return (
            rotate(query_lin, cosine_table, sine_table),
            rotate(key_lin, cosine_table, sine_table),
        )

    (query_rot, key_rot), turn_back = jax.vjp(
        turn_pair, merged_lin[..., :head_dim], merged_lin[..., head_dim : 2 * head_dim]
    )
    query_low = query_rot.astype(jnp.bfloat16)
    key_low = key_rot.astype(jnp.bfloat16)
    value_low = merged_lin[..., 2 * head_dim :].astype(jnp.bfloat16)
    score_scale = head_dim ** (-0.5)
    block_rows = min(512, group_rows)
    block_count = group_rows // block_rows
    row_index = jnp.arange(group_rows, dtype=jnp.int32)

    def masked_scores(number):
        begin_row = number * block_rows
        end_row = begin_row + block_rows
        scores = (
            jnp.einsum(
                "qhd,khd->hqk",
                query_low[begin_row:end_row],
                key_low[:end_row],
                preferred_element_type=jnp.float32,
            )
            * score_scale
        )
        allowed = (row_index[None, :end_row] <= row_index[begin_row:end_row, None]) & (
            seg_ids[None, :end_row] == seg_ids[begin_row:end_row, None]
        )
        return jnp.where(allowed[None], scores, -1e30)

    head_blocks = []
    log_totals = []
    for number in range(block_count):
        end_row = (number + 1) * block_rows
        scores = masked_scores(number)
        peak_score = jnp.max(scores, axis=-1, keepdims=True)
        weights = jnp.exp(scores - peak_score)
        norm_total = jnp.sum(weights, axis=-1, keepdims=True)
        log_totals.append(peak_score + jnp.log(norm_total))
        prob_low = (weights / norm_total).astype(jnp.bfloat16)
        head_blocks.append(
            jnp.einsum(
                "hqk,khd->qhd", prob_low, value_low[:end_row], preferred_element_type=jnp.float32
            )
        )
    heads_flat = (
        jnp.concatenate(head_blocks, axis=0).astype(jnp.bfloat16).reshape(group_rows, attn_cols)
    )
    attn_part = jnp.einsum(
        "gc,dc->gd",
        heads_flat,
        w_dense,
        preferred_element_type=jnp.float32,
    )
    fc_pre = jnp.dot(normed_mlp, w_fc, preferred_element_type=jnp.float32) + my_bias_fc
    act_full, gelu_back = jax.vjp(exact_gelu, fc_pre)
    act_low = act_full.astype(jnp.bfloat16)
    mlp_part = jnp.einsum("gf,df->gd", act_low, w_proj, preferred_element_type=jnp.float32)
    branch_rows = scatter_pairs(attn_part + mlp_part, "tensor")
    block_out = (
        x_rows + branch_rows + bias_dense.astype(jnp.float32) + bias_proj.astype(jnp.float32)
    ).astype(jnp.bfloat16)
    grad_act = jnp.dot(cot_all, w_proj, preferred_element_type=jnp.float32)
    grad_proj = jnp.einsum("gd,gf->df", cot_all, act_low, preferred_element_type=jnp.float32)
    grad_pre = gelu_back(grad_act)[0].astype(jnp.bfloat16)
    grad_fc = jnp.einsum("gd,gf->df", normed_mlp, grad_pre, preferred_element_type=jnp.float32)
    fc_bias_part = jnp.sum(grad_pre, axis=0, dtype=jnp.float32)
    grad_normed_mlp = jnp.einsum("gf,df->gd", grad_pre, w_fc, preferred_element_type=jnp.float32)
    grad_heads = (
        jnp.dot(cot_all, w_dense, preferred_element_type=jnp.float32)
        .astype(jnp.bfloat16)
        .reshape(group_rows, head_count, head_dim)
    )
    grad_dense = jnp.einsum(
        "gd,gc->dc", cot_all, heads_flat, preferred_element_type=jnp.float32
    )
    grad_heads, grad_fc, grad_proj = lax.optimization_barrier((grad_heads, grad_fc, grad_proj))
    query_grads = []
    grad_key = jnp.zeros((group_rows, head_count, head_dim), jnp.float32)
    grad_value = jnp.zeros((group_rows, head_count, head_dim), jnp.float32)
    for number in range(block_count):
        begin_row = number * block_rows
        end_row = begin_row + block_rows
        probs = jnp.exp(masked_scores(number) - log_totals[number])
        heads_blk = grad_heads[begin_row:end_row]
        grad_probs = jnp.einsum(
            "qhd,khd->hqk", heads_blk, value_low[:end_row], preferred_element_type=jnp.float32
        )
        row_delta = jnp.sum(probs * grad_probs, axis=-1, keepdims=True)
        grad_scores = (probs * (grad_probs - row_delta)).astype(jnp.bfloat16)
        query_grads.append(
            jnp.einsum(
                "hqk,khd->qhd", grad_scores, key_low[:end_row], preferred_element_type=jnp.float32
            )
            * score_scale
        )
        grad_key = grad_key.at[:end_row].add(
            jnp.einsum(
                "hqk,qhd->khd",
                grad_scores,
                query_low[begin_row:end_row],
                preferred_element_type=jnp.float32,
            )
            * score_scale
        )
        grad_value = grad_value.at[:end_row].add(
            jnp.einsum(
                "hqk,qhd->khd",
                probs.astype(jnp.bfloat16),
                heads_blk,
                preferred_element_type=jnp.float32,
            )
        )
    grad_query = jnp.concatenate(query_grads, axis=0)
    grad_query_lin, grad_key_lin = turn_back((grad_query, grad_key))
    grad_merged = (
        jnp.concatenate([grad_query_lin, grad_key_lin, grad_value], axis=-1)
        .astype(jnp.bfloat16)
        .reshape(group_rows, qkv_cols)
    )
    grad_qkv = jnp.einsum(
        "gd,gc->dc", normed_attn, grad_merged, preferred_element_type=jnp.float32
    )
    qkv_bias_part = jnp.sum(grad_merged, axis=0, dtype=jnp.float32)
    grad_normed_attn = jnp.einsum(
        "gc,dc->gd",
        grad_merged,
        w_qkv,
        preferred_element_type=jnp.float32,
    )
    cot_rows = out_grad.astype(jnp.float32)
    local_attn, local_mlp = (
        scatter_pairs(grad_normed_attn, "tensor"),
        scatter_pairs(grad_normed_mlp, "tensor"),
    )
    grad_x, grad_gain_attn, grad_shift_attn, grad_gain_mlp, grad_shift_mlp = norm_back(
        (local_attn, local_mlp)
    )
    input_grad = cot_rows + grad_x
    cot_sums = jnp.sum(cot_rows, axis=0)
    full_qkv_bias = lax.dynamic_update_slice_in_dim(
        jnp.zeros((qkv_cols * tensor_count,), jnp.float32),
        qkv_bias_part,
        tensor_index * qkv_cols,
        0,
    )
    full_fc_bias = lax.dynamic_update_slice_in_dim(
        jnp.zeros((hidden_units * tensor_count,), jnp.float32),
        fc_bias_part,
        tensor_index * hidden_units,
        0,
    )
    owners = lax.axis_size("dp") * tensor_count
    small_list = (
        grad_gain_attn,
        grad_shift_attn,
        grad_gain_mlp,
        grad_shift_mlp,
        full_qkv_bias,
        cot_sums,
        full_fc_bias,
    )
    small_packed = jnp.concatenate([item.reshape(owners, -1) for item in small_list], axis=1)
    small_packed = scatter_pairs(small_packed, "dp", 0, jnp.float32)
    small_packed = scatter_pairs(small_packed, "tensor", 0, jnp.float32).reshape(-1)
    small_sums = []
    begin = 0
    for item in small_list:
        count = item.shape[0] // owners
        small_sums.append(small_packed[begin : begin + count])
        begin += count
    third = qkv_cols // 3
    sum_qkv = jnp.concatenate(
        [
            scatter_pairs(grad_qkv[:, turn * third : (turn + 1) * third], "dp", turn)
            for turn in range(3)
        ],
        axis=1,
    )
    large_sums = (
        sum_qkv.reshape(qkv_weight.shape),
        scatter_pairs(grad_dense, "dp", 2).reshape(dense_weight.shape),
        scatter_pairs(grad_fc, "dp", 1),
        scatter_pairs(grad_proj, "dp", 2),
    )
    return (
        block_out,
        input_grad,
        small_sums[0],
        small_sums[1],
        small_sums[2],
        small_sums[3],
        large_sums[0],
        small_sums[4],
        large_sums[1],
        small_sums[5],
        large_sums[2],
        small_sums[6],
        large_sums[3],
        small_sums[5],
    )


def solution(mesh):
    in_specs = (
        P(("dp", "tensor"), None),
        P(("dp", "tensor"), None),
        P("dp", None),
        P("dp"),
        P("dp"),
        P("dp"),
        P("dp"),
        P("dp", "tensor", None),
        P("dp"),
        P("dp", "tensor", None),
        P("dp"),
        P("dp", "tensor"),
        P("dp"),
        P("dp", "tensor"),
        P("dp"),
    )
    out_specs = (
        P(("dp", "tensor"), None),
        P(("dp", "tensor"), None),
        P(("dp", "tensor")),
        P(("dp", "tensor")),
        P(("dp", "tensor")),
        P(("dp", "tensor")),
        P("dp", "tensor", None),
        P(("dp", "tensor")),
        P("dp", "tensor", None),
        P(("dp", "tensor")),
        P("dp", "tensor"),
        P(("dp", "tensor")),
        P("dp", "tensor"),
        P(("dp", "tensor")),
    )
    return jax.shard_map(body, mesh=mesh, in_specs=in_specs, out_specs=out_specs, check_vma=False)
```
